32 devices in a mesh: depth: 2 (over y), row: 4 (over x, core), col: 4 (over z).
Axes of the slice: x: 2, y: 2, z: 4, core: 2. Of those that a mesh axis runs over, the one named last changes fastest.
Arguments:
- normed: bfloat16 [1024, 6144], P(('depth', 'col'), 'row'), may hold values from -6 to 6
- positions: int32 [1024], P(('depth', 'col')), may hold values from 0 to 1567, as said below
- cotangent: bfloat16 [1024, 6144], P(('depth', 'col'), 'row'), may hold values from -5 to 5
- w_in: bfloat16 [6144, 12288], P('row', 'col'), may hold values from -0.078125 to 0.078125
- b_in: float32 [12288], P('col'), may hold values from -4 to 4
- w_out: bfloat16 [12288, 6144], P('col', 'row'), may hold values from -0.0546875 to 0.0546875
Outputs:
- d_normed: bfloat16 [1024, 6144], P(('depth', 'col'), 'row')
- d_w_in: float32 [6144, 12288], P('row', 'col')
- d_b_in: float32 [12288], P('col')
- d_w_out: float32 [12288, 6144], P('col', 'row')
The draws below stay inside these ranges and needn't reach their ends.
Inputs may be any that keep to these rules, and one draw needn't show every extreme that they name: positions holds 4 clips of 256 consecutive tokens; in each clip the same 256 // 8 of the 196 spatial places (ascending, always including places 0 and 195) are kept in each of the 8 frames, position = frame * 196 + place, frames ascending.
All inputs are finite; a program needn't handle non-finite values.
Results may differ from the reference program's by a relative error of at most 0.03.
Values may be sent and summed in bfloat16 or wider, within the bound.
A program may use at most 192 MiB of HBM per device.

```python
import jax
import jax.numpy as jnp
from jax import lax

D = 6144
FF = 12288
VIS = 256
TOKENS = 1024
N_COL = 4


def draw_positions(key, part):
    key = jax.random.fold_in(key, 7)
    keep = VIS // 8
    clip_keys = jax.random.split(key, TOKENS // VIS)

    def one_clip(clip_key):
        inner = (jax.random.permutation(clip_key, 194)[:keep - 2] + 1).astype(jnp.int32)
        ends = jnp.array([0, 195], dtype=jnp.int32)
        chosen = jnp.sort(jnp.concatenate([ends, inner])).astype(jnp.int32)
        frames = jnp.arange(8, dtype=jnp.int32)[:, None] * 196
        return (frames + chosen[None, :]).reshape(-1)
    return jax.vmap(one_clip)(clip_keys).reshape(-1).astype(jnp.int32)


def level_of(key, extent, cuts, smallest, high):
    factor_of = 1.0
    for axis_at, parts in cuts:
        steps = jax.random.uniform(jax.random.fold_in(jax.random.fold_in(key, 6), axis_at), (parts,), jnp.float32, smallest / len(cuts), high / len(cuts))
        factor_of = factor_of * jnp.repeat(jnp.exp(steps), extent[axis_at] // parts).reshape((-1,) + (1,) * (len(extent) - 1 - axis_at))
    return factor_of


def gaussian(stream_key, dims, deviation, limit, shards=(), kind=jnp.bfloat16):
    drawn = deviation * jax.random.normal(stream_key, dims, jnp.float32)
    if shards:
        drawn = drawn * level_of(stream_key, dims, shards, -0.22, 0.18)
    return jnp.clip(drawn, -limit, limit).astype(kind)


def setup_inputs(seed: int = 0) -> dict:
    key_list = jax.random.split(jax.random.key(seed), 7)
    normed = gaussian(key_list[0], (TOKENS, D), 1.0, 6.0, ((0, 8), (1, 4)))
    positions = draw_positions(jax.random.fold_in(key_list[6], 71), 0)
    cotangent = gaussian(key_list[2], (TOKENS, D), (2.0 * TOKENS ** -0.25), 5.0, ((0, 8), (1, 4)))
    w_in = gaussian(key_list[3], (D, FF), D ** -0.5, 0.078125, ((0, 4), (1, 4)))
    b_in = gaussian(key_list[4], (FF,), 1.0, 4.0, ((0, 4),), jnp.float32)
    w_out = gaussian(key_list[5], (FF, D), FF ** -0.5, 0.0546875, ((0, 4), (1, 4)))
    return dict(normed=normed, positions=positions, cotangent=cotangent, w_in=w_in, b_in=b_in, w_out=w_out)


coeff = 0.7978845608028654


def sincos(positions, first, width):
    places = positions.astype(jnp.float32)[:, None]
    column = first + jnp.arange(width, dtype=jnp.int32)
    expo = (2 * (column // 2)).astype(jnp.float32) / jnp.float32(D)
    freq = jnp.power(jnp.float32(10000.0), -expo)
    angle = places * freq[None, :]
    return jnp.where((column % 2 == 0)[None, :], jnp.sin(angle), jnp.cos(angle))


def gelu_pair(value):
    inner = coeff * (value + 0.044715 * value * value * value)
    slope = jnp.tanh(inner)
    out = 0.5 * value * (1.0 + slope)
    grad = 0.5 * (1.0 + slope) + 0.5 * value * (1.0 - slope * slope) * coeff * (1.0 + 3.0 * 0.044715 * value * value)
    return out, grad


def reference(normed, positions, cotangent, w_in, b_in, w_out):
    inputs = (normed.astype(jnp.float32) + sincos(positions, 0, D)).astype(jnp.bfloat16)
    pre = jnp.dot(inputs, w_in, preferred_element_type=jnp.float32) + b_in.astype(jnp.float32)
    act_f, slope = gelu_pair(pre)
    act = act_f.astype(jnp.bfloat16)
    d_act = jnp.dot(cotangent, w_out.T, preferred_element_type=jnp.float32)
    d_pre = (d_act * slope).astype(jnp.bfloat16)
    d_w_out = jnp.dot(act.T, cotangent, preferred_element_type=jnp.float32)
    d_w_in = jnp.dot(inputs.T, d_pre, preferred_element_type=jnp.float32)
    d_b_in = jnp.sum(d_pre.astype(jnp.float32), axis=0)
    block = FF // N_COL
    grad_blocks = d_pre.reshape(TOKENS, N_COL, block).transpose(1, 0, 2)
    weight_blocks = w_in.reshape(D, N_COL, block).transpose(1, 0, 2)

    def add_block(total, pair):
        part = jnp.dot(pair[0], pair[1].T, preferred_element_type=jnp.float32).astype(jnp.bfloat16)
        return total + part.astype(jnp.float32), None

    total, unused = lax.scan(add_block, jnp.zeros((TOKENS, D), jnp.float32), (grad_blocks, weight_blocks))
    d_normed = total.astype(jnp.bfloat16)
    return d_normed, d_w_in, d_b_in, d_w_out
```

```python
import functools
import math

import jax
import jax.numpy as jnp
from jax import lax
from jax.experimental import pallas as pl
from jax.experimental.pallas import tpu as pltpu
from jax.sharding import PartitionSpec as P

D = 6144
MESH = pl.DeviceIdType.MESH


coeff = 0.7978845608028654


def sincos(positions, first, width):
    places = positions.astype(jnp.float32)[:, None]
    column = first + jnp.arange(width, dtype=jnp.int32)
    expo = (2 * (column // 2)).astype(jnp.float32) / jnp.float32(D)
    freq = jnp.power(jnp.float32(10000.0), -expo)
    angle = places * freq[None, :]
    return jnp.where((column % 2 == 0)[None, :], jnp.sin(angle), jnp.cos(angle))


def gelu_pair(value):
    inner = coeff * (value + 0.044715 * value * value * value)
    slope = jnp.tanh(inner)
    out = 0.5 * value * (1.0 + slope)
    grad = 0.5 * (1.0 + slope) + 0.5 * value * (1.0 - slope * slope) * coeff * (
        1.0 + 3.0 * 0.044715 * value * value
    )
    return (out, grad)


def kernel(
    n_row, n_col,
    x_ref, c_ref, win_ref, wout_ref, b_ref,
    x_all, c_all, a_all, g_all,
    part, half, far,
    s_right, s_left, r_line, s_deep, r_deep,
    s_pair, r_pair, s_far, r_far,
    s_gx, r_gx, s_gy, r_gy, s_gyx, r_gyx, s_sib, r_sib,
):
    d, r, k = lax.axis_index("depth"), lax.axis_index("row"), lax.axis_index("col")
    nx = n_row // 2
    px, core = lax.div(r, 2), lax.rem(r, 2)
    sib = 2 * px + (1 - core)
    other = 1 - d
    block, hidden = x_ref.shape[0], win_ref.shape[1]
    sub = block // n_row
    tile = math.gcd(hidden, 768)
    tiles = hidden // tile
    low = jnp.minimum(k, n_col - 1 - k)
    ins, outs = (x_all, c_all), (a_all, g_all)
    sent = []

    def peer(i):
        return lax.rem(px + i, nx)

    def origin(i):
        return lax.rem(px + nx - i, nx)

    def remote(src, dst, send, recv, **where):
        return pltpu.make_async_remote_copy(
            src_ref=src, dst_ref=dst, send_sem=send, recv_sem=recv,
            device_id=where, device_id_type=MESH,
        )

    def go(*args, **where):
        copy = remote(*args, **where)
        copy.start()
        sent.append(copy)

    def which(s):
        if s == 0:
            return k
        near = k - (s + 1) // 2 if s % 2 else k + s // 2
        rest = jnp.where(2 * k < n_col - 1, k + (s - low), k - (s - low))
        return jnp.where(s <= 2 * low, near, rest)

    def line(arr, b, right):
        ref = ins[arr].at[b]
        if right:
            return remote(ref, ref, s_right.at[arr, b], r_line.at[arr, b], col=jnp.minimum(k + 1, n_col - 1))
        return remote(ref, ref, s_left.at[arr, b], r_line.at[arr, b], col=jnp.maximum(k - 1, 0))

    def deep(arr, b):
        return remote(ins[arr].at[b], ins[arr].at[n_col + b], s_deep.at[arr, b], r_deep.at[arr, b], depth=other)

    def forward(b):
        @pl.when(jnp.logical_and(b <= k, k < n_col - 1))
        def _():
            for arr in (0, 1):
                line(arr, b, True).start()

        @pl.when(jnp.logical_and(b >= k, k > 0))
        def _():
            for arr in (0, 1):
                line(arr, b, False).start()

        for arr in (0, 1):
            deep(arr, b).start()

    def arrive(s):
        b = which(s)
        for arr in (0, 1):
            line(arr, b, True).wait_recv()
        forward(b)

    def project(s):
        b = which(s)
        for arr in (0, 1):

            def body(i, carry):
                cols = pl.ds(pl.multiple_of(i * tile, tile), tile)
                if arr == 0:
                    acc = jnp.dot(x_all[b], win_ref[:, cols], preferred_element_type=jnp.float32)
                else:
                    acc = lax.dot_general(
                        c_all[b], wout_ref[cols, :], (((1,), (1,)), ((), ())),
                        preferred_element_type=jnp.float32,
                    )
                acc = acc.astype(jnp.bfloat16)
                for p in range(nx):
                    for q in (0, 1):
                        at = (2 * p + q) * sub
                        part[s, arr, q, p, :, cols] = acc[at : at + sub]
                return carry

            lax.fori_loop(0, tiles, body, 0)
            go(part.at[s, arr, 1 - core], half.at[s, arr], s_pair.at[s, arr], r_pair.at[s, arr], row=sib)

    def pair_sum(s):
        for arr in (0, 1):
            remote(
                part.at[s, arr, 1 - core], half.at[s, arr], s_pair.at[s, arr], r_pair.at[s, arr], row=sib
            ).wait_recv()

            def body(i, carry):
                cols = pl.ds(pl.multiple_of(i * tile, tile), tile)
                for p in range(nx):
                    mine = part[s, arr, core, p, :, cols].astype(jnp.float32)
                    theirs = half[s, arr, p, :, cols].astype(jnp.float32)
                    half[s, arr, p, :, cols] = (mine + theirs).astype(jnp.bfloat16)
                return carry

            lax.fori_loop(0, tiles, body, 0)
            for i in range(1, nx):
                go(
                    half.at[s, arr, peer(i)], far.at[s, arr, i - 1],
                    s_far.at[s, arr, i - 1], r_far.at[s, arr, i - 1], row=2 * peer(i) + core,
                )

    def finish(s):
        b = which(s)
        for arr in (0, 1):
            for i in range(1, nx):
                remote(
                    half.at[s, arr, peer(i)], far.at[s, arr, i - 1],
                    s_far.at[s, arr, i - 1], r_far.at[s, arr, i - 1], row=2 * peer(i) + core,
                ).wait_recv()

        def body(i, carry):
            cols = pl.ds(pl.multiple_of(i * tile, tile), tile)
            total = []
            for arr in (0, 1):
                value = half[s, arr, px, :, cols].astype(jnp.float32)
                for j in range(1, nx):
                    value = value + far[s, arr, j - 1, :, cols].astype(jnp.float32)
                total.append(value)
            act, slope = gelu_pair(total[0] + b_ref[:, cols])
            a_all[b, r, :, cols] = act.astype(jnp.bfloat16)
            g_all[b, r, :, cols] = (total[1] * slope).astype(jnp.bfloat16)
            return carry

        lax.fori_loop(0, tiles, body, 0)
        for arr in (1, 0):
            own = outs[arr].at[b, r]
            go(own, outs[arr].at[n_col + b, r], s_gy.at[s, arr], r_gy.at[s, arr], depth=other)
        for arr in (1, 0):
            own = outs[arr].at[b, r]
            for i in range(1, nx):
                go(own, own, s_gx.at[s, arr, i - 1], r_gx.at[s, arr, i - 1], row=2 * peer(i) + core)
            go(own, own, s_sib.at[s, arr, 0], r_sib.at[s, arr, 0], row=sib)

    def got(ref, recv):
        remote(ref, ref, s_sib.at[0, 0, 0], recv, row=sib).wait_recv()

    def relay(s):
        b = which(s)
        for arr in (1, 0):
            far_own = outs[arr].at[n_col + b, r]
            got(far_own, r_gy.at[s, arr])
            for i in range(1, nx):
                go(far_own, far_own, s_gyx.at[s, arr, i - 1], r_gyx.at[s, arr, i - 1], row=2 * peer(i) + core)
            go(far_own, far_own, s_sib.at[s, arr, nx], r_sib.at[s, arr, nx], row=sib)
        for arr in (1, 0):
            for i in range(1, nx):
                piece = outs[arr].at[b, 2 * origin(i) + core]
                got(piece, r_gx.at[s, arr, i - 1])
                go(piece, piece, s_sib.at[s, arr, i], r_sib.at[s, arr, i], row=sib)

    def relay_last(s):
        b = which(s)
        for arr in (1, 0):
            for i in range(1, nx):
                piece = outs[arr].at[n_col + b, 2 * origin(i) + core]
                got(piece, r_gyx.at[s, arr, i - 1])
                go(piece, piece, s_sib.at[s, arr, nx + i], r_sib.at[s, arr, nx + i], row=sib)

    barrier = pltpu.get_barrier_semaphore()
    pl.semaphore_signal(barrier, inc=1, device_id={"row": sib}, device_id_type=MESH)
    pl.semaphore_signal(barrier, inc=1, device_id={"depth": other}, device_id_type=MESH)
    for i in range(1, nx):
        pl.semaphore_signal(barrier, inc=1, device_id={"row": 2 * peer(i) + core}, device_id_type=MESH)

    @pl.when(k > 0)
    def _():
        pl.semaphore_signal(barrier, inc=1, device_id={"col": jnp.maximum(k - 1, 0)}, device_id_type=MESH)

    @pl.when(k < n_col - 1)
    def _():
        pl.semaphore_signal(barrier, inc=1, device_id={"col": jnp.minimum(k + 1, n_col - 1)}, device_id_type=MESH)

    x_all[k] = x_ref[...]
    c_all[k] = c_ref[...]
    ends = jnp.where(k > 0, 1, 0) + jnp.where(k < n_col - 1, 1, 0)
    pl.semaphore_wait(barrier, 2 + (nx - 1) + ends)

    forward(k)
    for s in range(n_col):
        if s % 2:
            arrive(s)
            if s + 1 < n_col:
                pl.when(s + 1 <= 2 * low)(functools.partial(arrive, s + 1))
        elif s:
            pl.when(s > 2 * low)(functools.partial(arrive, s))
        project(s)
        if s >= 1:
            finish(s - 1)
        pair_sum(s)
        if s >= 2:
            relay(s - 2)
        if s >= 3:
            relay_last(s - 3)
    finish(n_col - 1)
    for s in range(max(n_col - 2, 0), n_col):
        relay(s)
        if s >= 1:
            relay_last(s - 1)
    relay_last(n_col - 1)

    for s in range(n_col):
        b = which(s)
        for arr in (0, 1):
            for i in range(nx):
                at = 2 * origin(i) + (1 - core)
                got(outs[arr].at[b, at], r_sib.at[s, arr, i])
                got(outs[arr].at[n_col + b, at], r_sib.at[s, arr, nx + i])

    for b in range(n_col):
        for arr in (0, 1):
            deep(arr, b).wait()

            @pl.when(jnp.logical_and(b <= k, k < n_col - 1))
            def _():
                line(arr, b, True).wait_send()

            @pl.when(jnp.logical_and(b >= k, k > 0))
            def _():
                line(arr, b, False).wait_send()

    for copy in sent:
        copy.wait_send()


def exchange(n_row, n_col, inputs, cotangent, w_in, w_out, b_in):
    block, width = inputs.shape
    hidden = w_in.shape[1]
    nx, sub = n_row // 2, block // n_row
    kind = jnp.bfloat16
    wide = jax.ShapeDtypeStruct((2 * n_col, block, width), kind)
    deep = jax.ShapeDtypeStruct((2 * n_col, n_row, sub, hidden), kind)
    vmem = pl.BlockSpec(memory_space=pltpu.VMEM)
    sem = lambda *shape: pltpu.SemaphoreType.DMA(shape)
    flops = 4 * n_col * block * width * hidden
    return pl.pallas_call(
        functools.partial(kernel, n_row, n_col),
        out_shape=(wide, wide, deep, deep),
        in_specs=[vmem] * 5,
        out_specs=(vmem,) * 4,
        scratch_shapes=[
            pltpu.VMEM((n_col, 2, 2, nx, sub, hidden), kind),
            pltpu.VMEM((n_col, 2, nx, sub, hidden), kind),
            pltpu.VMEM((n_col, 2, nx - 1, sub, hidden), kind),
        ]
        + [sem(2, n_col)] * 5
        + [sem(n_col, 2)] * 2
        + [sem(n_col, 2, nx - 1)] * 2
        + [sem(n_col, 2, nx - 1)] * 2
        + [sem(n_col, 2)] * 2
        + [sem(n_col, 2, nx - 1)] * 2
        + [sem(n_col, 2, 2 * nx)] * 2,
        compiler_params=pltpu.CompilerParams(
            collective_id=0, has_side_effects=True, vmem_limit_bytes=60 * 2**20
        ),
        cost_estimate=pl.CostEstimate(
            flops=flops, bytes_accessed=4 * width * hidden, transcendentals=block * hidden
        ),
    )(inputs, cotangent, w_in, w_out, b_in)


def on_device(n_row, n_col, normed, positions, cotangent, w_in, b_in, w_out):
    width, hidden = w_in.shape
    first = lax.axis_index("row") * width
    inputs = (normed.astype(jnp.float32) + sincos(positions, first, width)).astype(jnp.bfloat16)
    x_all, c_all, a_all, g_all = exchange(
        n_row, n_col, inputs, cotangent, w_in, w_out, b_in.reshape(1, hidden)
    )
    rows = x_all.shape[0] * x_all.shape[1]
    grads = g_all.reshape(rows, hidden)
    d_normed = lax.psum_scatter(
        lax.dot_general(
            grads[: rows // 2], w_in, (((1,), (1,)), ((), ())), preferred_element_type=jnp.float32
        ).astype(jnp.bfloat16),
        "col",
        scatter_dimension=0,
        tiled=True,
    )
    contract = (((0,), (0,)), ((), ()))
    d_w_out = lax.dot_general(
        a_all.reshape(rows, hidden), c_all.reshape(rows, width), contract,
        preferred_element_type=jnp.float32,
    )
    d_w_in = lax.dot_general(
        x_all.reshape(rows, width), grads, contract, preferred_element_type=jnp.float32
    )
    d_b_in = jnp.sum(grads.astype(jnp.float32), axis=0)
    return (d_normed, d_w_in, d_b_in, d_w_out)


def solution(mesh):
    placed = (
        P(("depth", "col"), "row"),
        P(("depth", "col")),
        P(("depth", "col"), "row"),
        P("row", "col"),
        P("col"),
        P("col", "row"),
    )
    return jax.shard_map(
        functools.partial(on_device, mesh.shape["row"], mesh.shape["col"]),
        mesh=mesh,
        in_specs=placed,
        out_specs=(P(("depth", "col"), "row"), P("row", "col"), P("col"), P("col", "row")),
        check_vma=False,
    )
```

```python
import functools
import math

import jax
import jax.numpy as jnp
from jax import lax
from jax.experimental import pallas as pl
from jax.experimental.pallas import tpu as pltpu
from jax.sharding import PartitionSpec as P

D = 6144
MESH = pl.DeviceIdType.MESH


coeff = 0.7978845608028654


def sincos(positions, first, width):
    places = positions.astype(jnp.float32)[:, None]
    column = first + jnp.arange(width, dtype=jnp.int32)
    expo = (2 * (column // 2)).astype(jnp.float32) / jnp.float32(D)
    freq = jnp.power(jnp.float32(10000.0), -expo)
    angle = places * freq[None, :]
    return jnp.where((column % 2 == 0)[None, :], jnp.sin(angle), jnp.cos(angle))


def gelu_pair(value):
    inner = coeff * (value + 0.044715 * value * value * value)
    slope = jnp.tanh(inner)
    out = 0.5 * value * (1.0 + slope)
    grad = 0.5 * (1.0 + slope) + 0.5 * value * (1.0 - slope * slope) * coeff * (
        1.0 + 3.0 * 0.044715 * value * value
    )
    return (out, grad)


def kernel(
    n_row, n_col,
    x_ref, c_ref, win_hbm, wout_hbm, b_ref,
    x_out, c_out, a_out, g_out, d_out,
    x_all, c_all, a_all, g_all, win_ref, wout_ref,
    part, half, far, share, shares,
    s_right, s_left, r_line, s_deep, r_deep,
    s_pair, r_pair, s_far, r_far,
    s_gx, r_gx, s_gy, r_gy, s_gyx, r_gyx, s_sib, r_sib,
    s_share, r_share, w_sem, o_in, o_mid,
):
    d, r, k = lax.axis_index("depth"), lax.axis_index("row"), lax.axis_index("col")
    nx = n_row // 2
    px, core = lax.div(r, 2), lax.rem(r, 2)
    sib = 2 * px + (1 - core)
    other = 1 - d
    block, width = x_ref.shape
    hidden = win_ref.shape[1]
    sub = block // n_row
    tile = math.gcd(hidden, 768)
    tiles = hidden // tile
    low = jnp.minimum(k, n_col - 1 - k)
    ins, outs = (x_all, c_all), (a_all, g_all)
    ins_out, outs_out = (x_out, c_out), (a_out, g_out)
    sent, kept = [], []
    weights = [
        pltpu.make_async_copy(win_hbm, win_ref, w_sem.at[0]),
        pltpu.make_async_copy(wout_hbm, wout_ref, w_sem.at[1]),
    ]
    for copy in weights:
        copy.start()

    def keep(src, dst, sem):
        copy = pltpu.make_async_copy(src, dst, sem)
        copy.start()
        kept.append(copy)

    def peer(i):
        return lax.rem(px + i, nx)

    def origin(i):
        return lax.rem(px + nx - i, nx)

    def remote(src, dst, send, recv, **where):
        return pltpu.make_async_remote_copy(
            src_ref=src, dst_ref=dst, send_sem=send, recv_sem=recv,
            device_id=where, device_id_type=MESH,
        )

    def go(*args, **where):
        copy = remote(*args, **where)
        copy.start()
        sent.append(copy)

    def which(s):
        if s == 0:
            return k
        near = k - (s + 1) // 2 if s % 2 else k + s // 2
        rest = jnp.where(2 * k < n_col - 1, k + (s - low), k - (s - low))
        return jnp.where(s <= 2 * low, near, rest)

    def line(arr, b, right):
        ref = ins[arr].at[b]
        if right:
            return remote(ref, ref, s_right.at[arr, b], r_line.at[arr, b], col=jnp.minimum(k + 1, n_col - 1))
        return remote(ref, ref, s_left.at[arr, b], r_line.at[arr, b], col=jnp.maximum(k - 1, 0))

    def deep(arr, b):
        return remote(ins[arr].at[b], ins[arr].at[n_col + b], s_deep.at[arr, b], r_deep.at[arr, b], depth=other)

    def forward(b):
        @pl.when(jnp.logical_and(b <= k, k < n_col - 1))
        def _():
            for arr in (0, 1):
                line(arr, b, True).start()

        @pl.when(jnp.logical_and(b >= k, k > 0))
        def _():
            for arr in (0, 1):
                line(arr, b, False).start()

        for arr in (0, 1):
            deep(arr, b).start()

    def arrive(s):
        b = which(s)
        for arr in (0, 1):
            line(arr, b, True).wait_recv()
        forward(b)

    def project(s):
        b = which(s)
        for arr in (0, 1):
            if s == 0:
                weights[arr].wait()

            def body(i, carry):
                cols = pl.ds(pl.multiple_of(i * tile, tile), tile)
                if arr == 0:
                    acc = jnp.dot(x_all[b], win_ref[:, cols], preferred_element_type=jnp.float32)
                else:
                    acc = lax.dot_general(
                        c_all[b], wout_ref[cols, :], (((1,), (1,)), ((), ())),
                        preferred_element_type=jnp.float32,
                    )
                acc = acc.astype(jnp.bfloat16)
                for p in range(nx):
                    for q in (0, 1):
                        at = (2 * p + q) * sub
                        part[s, arr, q, p, :, cols] = acc[at : at + sub]
                return carry

            lax.fori_loop(0, tiles, body, 0)
            go(part.at[s, arr, 1 - core], half.at[s, arr], s_pair.at[s, arr], r_pair.at[s, arr], row=sib)

    def pair_sum(s):
        for arr in (0, 1):
            remote(
                part.at[s, arr, 1 - core], half.at[s, arr], s_pair.at[s, arr], r_pair.at[s, arr], row=sib
            ).wait_recv()

            def body(i, carry):
                cols = pl.ds(pl.multiple_of(i * tile, tile), tile)
                for p in range(nx):
                    mine = part[s, arr, core, p, :, cols].astype(jnp.float32)
                    theirs = half[s, arr, p, :, cols].astype(jnp.float32)
                    half[s, arr, p, :, cols] = (mine + theirs).astype(jnp.bfloat16)
                return carry

            lax.fori_loop(0, tiles, body, 0)
            for i in range(1, nx):
                go(
                    half.at[s, arr, peer(i)], far.at[s, arr, i - 1],
                    s_far.at[s, arr, i - 1], r_far.at[s, arr, i - 1], row=2 * peer(i) + core,
                )

    def finish(s):
        b = which(s)
        for arr in (0, 1):
            for i in range(1, nx):
                remote(
                    half.at[s, arr, peer(i)], far.at[s, arr, i - 1],
                    s_far.at[s, arr, i - 1], r_far.at[s, arr, i - 1], row=2 * peer(i) + core,
                ).wait_recv()

        def body(i, carry):
            cols = pl.ds(pl.multiple_of(i * tile, tile), tile)
            total = []
            for arr in (0, 1):
                value = half[s, arr, px, :, cols].astype(jnp.float32)
                for j in range(1, nx):
                    value = value + far[s, arr, j - 1, :, cols].astype(jnp.float32)
                total.append(value)
            act, slope = gelu_pair(total[0] + b_ref[:, cols])
            a_all[b, r, :, cols] = act.astype(jnp.bfloat16)
            g_all[b, r, :, cols] = (total[1] * slope).astype(jnp.bfloat16)
            return carry

        lax.fori_loop(0, tiles, body, 0)
        for arr in (1, 0):
            own = outs[arr].at[b, r]
            go(own, outs[arr].at[n_col + b, r], s_gy.at[s, arr], r_gy.at[s, arr], depth=other)
        for arr in (1, 0):
            own = outs[arr].at[b, r]
            for i in range(1, nx):
                go(own, own, s_gx.at[s, arr, i - 1], r_gx.at[s, arr, i - 1], row=2 * peer(i) + core)
            go(own, own, s_sib.at[s, arr, 0], r_sib.at[s, arr, 0], row=sib)

    def got(ref, recv):
        remote(ref, ref, s_sib.at[0, 0, 0], recv, row=sib).wait_recv()

    def relay(s):
        b = which(s)
        for arr in (1, 0):
            far_own = outs[arr].at[n_col + b, r]
            got(far_own, r_gy.at[s, arr])
            for i in range(1, nx):
                go(far_own, far_own, s_gyx.at[s, arr, i - 1], r_gyx.at[s, arr, i - 1], row=2 * peer(i) + core)
            go(far_own, far_own, s_sib.at[s, arr, nx], r_sib.at[s, arr, nx], row=sib)
        for arr in (1, 0):
            for i in range(1, nx):
                piece = outs[arr].at[b, 2 * origin(i) + core]
                got(piece, r_gx.at[s, arr, i - 1])
                go(piece, piece, s_sib.at[s, arr, i], r_sib.at[s, arr, i], row=sib)

    def relay_last(s):
        b = which(s)
        for arr in (1, 0):
            for i in range(1, nx):
                piece = outs[arr].at[n_col + b, 2 * origin(i) + core]
                got(piece, r_gyx.at[s, arr, i - 1])
                go(piece, piece, s_sib.at[s, arr, nx + i], r_sib.at[s, arr, nx + i], row=sib)

    def back(s):
        b = which(s)
        for i in range(nx):
            got(g_all.at[b, 2 * origin(i) + (1 - core)], r_sib.at[s, 1, i])
        step = math.gcd(width, 768)

        def body(i, carry):
            cols = pl.ds(pl.multiple_of(i * step, step), step)
            acc = lax.dot_general(
                g_all[b].reshape(block, hidden), win_ref[cols, :], (((1,), (1,)), ((), ())),
                preferred_element_type=jnp.float32,
            )
            share[s, :, cols] = acc.astype(jnp.bfloat16)
            return carry

        lax.fori_loop(0, width // step, body, 0)
        if s:
            go(share.at[s], shares.at[k], s_share.at[s], r_share.at[k], col=b)

    barrier = pltpu.get_barrier_semaphore()
    pl.semaphore_signal(barrier, inc=1, device_id={"row": sib}, device_id_type=MESH)
    pl.semaphore_signal(barrier, inc=1, device_id={"depth": other}, device_id_type=MESH)
    for i in range(1, nx):
        pl.semaphore_signal(barrier, inc=1, device_id={"row": 2 * peer(i) + core}, device_id_type=MESH)

    for i in range(1, n_col):
        pl.semaphore_signal(barrier, inc=1, device_id={"col": lax.rem(k + i, n_col)}, device_id_type=MESH)

    x_all[k] = x_ref[...]
    c_all[k] = c_ref[...]
    pl.semaphore_wait(barrier, 2 + (nx - 1) + (n_col - 1))

    forward(k)
    for s in range(n_col):
        if s % 2:

            @pl.when(s <= 2 * low)
            def _():
                arrive(s)
                if s + 1 < n_col:
                    arrive(s + 1)

        if s >= 1:
            pl.when(jnp.logical_and(low > 0, s > 2 * low))(functools.partial(arrive, s))
            finish(s - 1)
            pl.when(low == 0)(functools.partial(arrive, s))
        project(s)
        pair_sum(s)
        if s >= 2:
            back(s - 2)
        if s >= 1:
            relay(s - 1)
        if s >= 2:
            relay_last(s - 2)
    for arr in (0, 1):
        keep(ins[arr].at[pl.ds(0, n_col)], ins_out[arr].at[pl.ds(0, n_col)], o_in.at[arr, n_col])
    finish(n_col - 1)
    if n_col >= 2:
        back(n_col - 2)
        relay_last(n_col - 2)
    relay(n_col - 1)
    back(n_col - 1)
    relay_last(n_col - 1)

    for s in range(n_col):
        b = which(s)
        for arr in (1, 0):
            for i in range(nx):
                at = 2 * origin(i) + (1 - core)
                if arr == 0:
                    got(outs[arr].at[b, at], r_sib.at[s, arr, i])
                got(outs[arr].at[n_col + b, at], r_sib.at[s, arr, nx + i])
            keep(outs[arr].at[b], outs_out[arr].at[b], o_mid.at[s, arr, 0])
            keep(outs[arr].at[n_col + b], outs_out[arr].at[n_col + b], o_mid.at[s, arr, 1])

    total = share[0].astype(jnp.float32)
    for s in range(1, n_col):
        b = which(s)
        remote(share.at[s], shares.at[b], s_share.at[s], r_share.at[b], col=b).wait_recv()
        total = total + shares[b].astype(jnp.float32)
    d_out[...] = total.astype(jnp.bfloat16)

    for b in range(n_col):
        for arr in (0, 1):
            deep(arr, b).wait()
            keep(ins[arr].at[n_col + b], ins_out[arr].at[n_col + b], o_in.at[arr, b])

            @pl.when(jnp.logical_and(b <= k, k < n_col - 1))
            def _():
                line(arr, b, True).wait_send()

            @pl.when(jnp.logical_and(b >= k, k > 0))
            def _():
                line(arr, b, False).wait_send()

    for copy in sent:
        copy.wait_send()
    for copy in kept:
        copy.wait()


def exchange(n_row, n_col, inputs, cotangent, w_in, w_out, b_in):
    block, width = inputs.shape
    hidden = w_in.shape[1]
    nx, sub = n_row // 2, block // n_row
    kind = jnp.bfloat16
    wide = jax.ShapeDtypeStruct((2 * n_col, block, width), kind)
    deep = jax.ShapeDtypeStruct((2 * n_col, n_row, sub, hidden), kind)
    vmem, hbm = pl.BlockSpec(memory_space=pltpu.VMEM), pl.BlockSpec(memory_space=pl.ANY)
    sem = lambda *shape: pltpu.SemaphoreType.DMA(shape)
    flops = 6 * n_col * block * width * hidden
    return pl.pallas_call(
        functools.partial(kernel, n_row, n_col),
        out_shape=(wide, wide, deep, deep, jax.ShapeDtypeStruct((block, width), kind)),
        in_specs=[vmem, vmem, hbm, hbm, vmem],
        out_specs=(hbm,) * 4 + (vmem,),
        scratch_shapes=[pltpu.VMEM(a.shape, kind) for a in (wide, wide, deep, deep, w_in, w_out)]
        + [
            pltpu.VMEM((n_col, 2, 2, nx, sub, hidden), kind),
            pltpu.VMEM((n_col, 2, nx, sub, hidden), kind),
            pltpu.VMEM((n_col, 2, nx - 1, sub, hidden), kind),
            pltpu.VMEM((n_col, block, width), kind),
            pltpu.VMEM((n_col, block, width), kind),
        ]
        + [sem(2, n_col)] * 5
        + [sem(n_col, 2)] * 2
        + [sem(n_col, 2, nx - 1)] * 2
        + [sem(n_col, 2, nx - 1)] * 2
        + [sem(n_col, 2)] * 2
        + [sem(n_col, 2, nx - 1)] * 2
        + [sem(n_col, 2, 2 * nx)] * 2
        + [sem(n_col)] * 2
        + [sem(2), sem(2, n_col + 1), sem(n_col, 2, 2)],
        compiler_params=pltpu.CompilerParams(
            collective_id=0, has_side_effects=True, vmem_limit_bytes=60 * 2**20
        ),
        cost_estimate=pl.CostEstimate(
            flops=flops, bytes_accessed=4 * width * hidden, transcendentals=block * hidden
        ),
    )(inputs, cotangent, w_in, w_out, b_in)


def on_device(n_row, n_col, normed, positions, cotangent, w_in, b_in, w_out):
    width, hidden = w_in.shape
    first = lax.axis_index("row") * width
    inputs = (normed.astype(jnp.float32) + sincos(positions, first, width)).astype(jnp.bfloat16)
    x_all, c_all, a_all, g_all, d_normed = exchange(
        n_row, n_col, inputs, cotangent, w_in, w_out, b_in.reshape(1, hidden)
    )
    rows = x_all.shape[0] * x_all.shape[1]
    grads = g_all.reshape(rows, hidden)
    contract = (((0,), (0,)), ((), ()))
    d_w_out = lax.dot_general(
        a_all.reshape(rows, hidden), c_all.reshape(rows, width), contract,
        preferred_element_type=jnp.float32,
    )
    d_w_in = lax.dot_general(
        x_all.reshape(rows, width), grads, contract, preferred_element_type=jnp.float32
    )
    d_b_in = jnp.sum(grads.astype(jnp.float32), axis=0)
    return (d_normed, d_w_in, d_b_in, d_w_out)


def solution(mesh):
    placed = (
        P(("depth", "col"), "row"),
        P(("depth", "col")),
        P(("depth", "col"), "row"),
        P("row", "col"),
        P("col"),
        P("col", "row"),
    )
    return jax.shard_map(
        functools.partial(on_device, mesh.shape["row"], mesh.shape["col"]),
        mesh=mesh,
        in_specs=placed,
        out_specs=(P(("depth", "col"), "row"), P("row", "col"), P("col"), P("col", "row")),
        check_vma=False,
    )
```

```python
import functools
import math

import jax
import jax.numpy as jnp
from jax import lax
from jax.experimental import pallas as pl
from jax.experimental.pallas import tpu as pltpu
from jax.sharding import PartitionSpec as P

D = 6144
MESH = pl.DeviceIdType.MESH


coeff = 0.7978845608028654


def sincos(positions, first, width):
    places = positions.astype(jnp.float32)[:, None]
    column = first + jnp.arange(width, dtype=jnp.int32)
    expo = (2 * (column // 2)).astype(jnp.float32) / jnp.float32(D)
    freq = jnp.power(jnp.float32(10000.0), -expo)
    angle = places * freq[None, :]
    return jnp.where((column % 2 == 0)[None, :], jnp.sin(angle), jnp.cos(angle))


def gelu_pair(value):
    inner = coeff * (value + 0.044715 * value * value * value)
    slope = jnp.tanh(inner)
    out = 0.5 * value * (1.0 + slope)
    grad = 0.5 * (1.0 + slope) + 0.5 * value * (1.0 - slope * slope) * coeff * (
        1.0 + 3.0 * 0.044715 * value * value
    )
    return (out, grad)


def kernel(
    n_row, n_col,
    x_ref, c_ref, win_hbm, wout_hbm, b_ref,
    x_out, c_out, a_out, g_out, d_out, bias,
    x_all, c_all, a_all, g_all, win_ref, wout_ref,
    part, half, far, share, shares,
    s_right, s_left, r_line, s_deep, r_deep,
    s_pair, r_pair, s_far, r_far,
    s_gx, r_gx, s_gy, r_gy, s_gyx, r_gyx, s_sib, r_sib,
    s_share, r_share, w_sem, o_in, o_mid,
):
    d, r, k = lax.axis_index("depth"), lax.axis_index("row"), lax.axis_index("col")
    nx = n_row // 2
    px, core = lax.div(r, 2), lax.rem(r, 2)
    sib = 2 * px + (1 - core)
    other = 1 - d
    block, width = x_ref.shape
    hidden = win_ref.shape[1]
    sub = block // n_row
    tile = math.gcd(hidden, 768)
    tiles = hidden // tile
    low = jnp.minimum(k, n_col - 1 - k)
    ins, outs = (x_all, c_all), (a_all, g_all)
    ins_out, outs_out = (x_out, c_out), (a_out, g_out)
    sent, kept = [], []
    weights = [
        pltpu.make_async_copy(win_hbm, win_ref, w_sem.at[0]),
        pltpu.make_async_copy(wout_hbm, wout_ref, w_sem.at[1]),
    ]
    for copy in weights:
        copy.start()

    def keep(src, dst, sem):
        copy = pltpu.make_async_copy(src, dst, sem)
        copy.start()
        kept.append(copy)

    def peer(i):
        return lax.rem(px + i, nx)

    def origin(i):
        return lax.rem(px + nx - i, nx)

    def remote(src, dst, send, recv, **where):
        return pltpu.make_async_remote_copy(
            src_ref=src, dst_ref=dst, send_sem=send, recv_sem=recv,
            device_id=where, device_id_type=MESH,
        )

    def go(*args, **where):
        copy = remote(*args, **where)
        copy.start()
        sent.append(copy)

    def which(s):
        if s == 0:
            return k
        near = k - (s + 1) // 2 if s % 2 else k + s // 2
        rest = jnp.where(2 * k < n_col - 1, k + (s - low), k - (s - low))
        return jnp.where(s <= 2 * low, near, rest)

    def line(arr, b, right):
        ref = ins[arr].at[b]
        if right:
            return remote(ref, ref, s_right.at[arr, b], r_line.at[arr, b], col=jnp.minimum(k + 1, n_col - 1))
        return remote(ref, ref, s_left.at[arr, b], r_line.at[arr, b], col=jnp.maximum(k - 1, 0))

    def deep(arr, b):
        return remote(ins[arr].at[b], ins[arr].at[n_col + b], s_deep.at[arr, b], r_deep.at[arr, b], depth=other)

    def forward(b):
        @pl.when(jnp.logical_and(b <= k, k < n_col - 1))
        def _():
            for arr in (0, 1):
                line(arr, b, True).start()

        @pl.when(jnp.logical_and(b >= k, k > 0))
        def _():
            for arr in (0, 1):
                line(arr, b, False).start()

    def cross(s):
        for arr in (0, 1):
            deep(arr, which(s)).start()

    def arrive(s):
        b = which(s)
        for arr in (0, 1):
            line(arr, b, True).wait_recv()
        forward(b)

    def project(s, *arrs):
        b = which(s)
        for arr in arrs:
            if s == 0:
                weights[arr].wait()

            def body(i, carry):
                cols = pl.ds(pl.multiple_of(i * tile, tile), tile)
                if arr == 0:
                    acc = jnp.dot(x_all[b], win_ref[:, cols], preferred_element_type=jnp.float32)
                else:
                    acc = lax.dot_general(
                        c_all[b], wout_ref[cols, :], (((1,), (1,)), ((), ())),
                        preferred_element_type=jnp.float32,
                    )
                acc = acc.astype(jnp.bfloat16)
                for p in range(nx):
                    for q in (0, 1):
                        at = (2 * p + q) * sub
                        part[s, arr, q, p, :, cols] = acc[at : at + sub]
                return carry

            lax.fori_loop(0, tiles, body, 0)
            go(part.at[s, arr, 1 - core], half.at[s, arr], s_pair.at[s, arr], r_pair.at[s, arr], row=sib)

    def pair_sum(s):
        for arr in (0, 1):
            remote(
                part.at[s, arr, 1 - core], half.at[s, arr], s_pair.at[s, arr], r_pair.at[s, arr], row=sib
            ).wait_recv()

            def body(i, carry):
                cols = pl.ds(pl.multiple_of(i * tile, tile), tile)
                for p in range(nx):
                    mine = part[s, arr, core, p, :, cols].astype(jnp.float32)
                    theirs = half[s, arr, p, :, cols].astype(jnp.float32)
                    half[s, arr, p, :, cols] = (mine + theirs).astype(jnp.bfloat16)
                return carry

            lax.fori_loop(0, tiles, body, 0)
            for i in range(1, nx):
                go(
                    half.at[s, arr, peer(i)], far.at[s, arr, i - 1],
                    s_far.at[s, arr, i - 1], r_far.at[s, arr, i - 1], row=2 * peer(i) + core,
                )

    def finish(s):
        b = which(s)
        for arr in (0, 1):
            for i in range(1, nx):
                remote(
                    half.at[s, arr, peer(i)], far.at[s, arr, i - 1],
                    s_far.at[s, arr, i - 1], r_far.at[s, arr, i - 1], row=2 * peer(i) + core,
                ).wait_recv()

        def body(i, carry):
            cols = pl.ds(pl.multiple_of(i * tile, tile), tile)
            total = []
            for arr in (0, 1):
                value = half[s, arr, px, :, cols].astype(jnp.float32)
                for j in range(1, nx):
                    value = value + far[s, arr, j - 1, :, cols].astype(jnp.float32)
                total.append(value)
            act, slope = gelu_pair(total[0] + b_ref[:, cols])
            a_all[b, r, :, cols] = act.astype(jnp.bfloat16)
            g_all[b, r, :, cols] = (total[1] * slope).astype(jnp.bfloat16)
            return carry

        lax.fori_loop(0, tiles, body, 0)
        for arr in (1, 0):
            own = outs[arr].at[b, r]
            go(own, outs[arr].at[n_col + b, r], s_gy.at[s, arr], r_gy.at[s, arr], depth=other)
        for arr in (1, 0):
            own = outs[arr].at[b, r]
            for i in range(1, nx):
                go(own, own, s_gx.at[s, arr, i - 1], r_gx.at[s, arr, i - 1], row=2 * peer(i) + core)
            go(own, own, s_sib.at[s, arr, 0], r_sib.at[s, arr, 0], row=sib)

    def got(ref, recv):
        remote(ref, ref, s_sib.at[0, 0, 0], recv, row=sib).wait_recv()

    def relay(s):
        b = which(s)
        for arr in (1, 0):
            far_own = outs[arr].at[n_col + b, r]
            got(far_own, r_gy.at[s, arr])
            for i in range(1, nx):
                go(far_own, far_own, s_gyx.at[s, arr, i - 1], r_gyx.at[s, arr, i - 1], row=2 * peer(i) + core)
            go(far_own, far_own, s_sib.at[s, arr, nx], r_sib.at[s, arr, nx], row=sib)
        for arr in (1, 0):
            for i in range(1, nx):
                piece = outs[arr].at[b, 2 * origin(i) + core]
                got(piece, r_gx.at[s, arr, i - 1])
                go(piece, piece, s_sib.at[s, arr, i], r_sib.at[s, arr, i], row=sib)

    def relay_last(s):
        b = which(s)
        for arr in (1, 0):
            for i in range(1, nx):
                piece = outs[arr].at[n_col + b, 2 * origin(i) + core]
                got(piece, r_gyx.at[s, arr, i - 1])
                go(piece, piece, s_sib.at[s, arr, nx + i], r_sib.at[s, arr, nx + i], row=sib)

    def add_bias(b):
        def body(i, carry):
            cols = pl.ds(pl.multiple_of(i * tile, tile), tile)
            rows = g_all[b, :, :, cols].astype(jnp.float32).reshape(block, tile)
            bias[:, cols] += jnp.sum(rows, axis=0, keepdims=True)
            return carry

        lax.fori_loop(0, tiles, body, 0)

    def back(s):
        b = which(s)
        for i in range(nx):
            got(g_all.at[b, 2 * origin(i) + (1 - core)], r_sib.at[s, 1, i])
        step = math.gcd(width, 768)

        def body(i, carry):
            cols = pl.ds(pl.multiple_of(i * step, step), step)
            acc = lax.dot_general(
                g_all[b].reshape(block, hidden), win_ref[cols, :], (((1,), (1,)), ((), ())),
                preferred_element_type=jnp.float32,
            )
            share[s, :, cols] = acc.astype(jnp.bfloat16)
            return carry

        lax.fori_loop(0, width // step, body, 0)
        add_bias(b)
        if s:
            go(share.at[s], shares.at[k], s_share.at[s], r_share.at[k], col=b)

    barrier = pltpu.get_barrier_semaphore()
    pl.semaphore_signal(barrier, inc=1, device_id={"row": sib}, device_id_type=MESH)
    pl.semaphore_signal(barrier, inc=1, device_id={"depth": other}, device_id_type=MESH)
    for i in range(1, nx):
        pl.semaphore_signal(barrier, inc=1, device_id={"row": 2 * peer(i) + core}, device_id_type=MESH)

    for i in range(1, n_col):
        pl.semaphore_signal(barrier, inc=1, device_id={"col": lax.rem(k + i, n_col)}, device_id_type=MESH)

    x_all[k] = x_ref[...]
    c_all[k] = c_ref[...]
    pl.semaphore_wait(barrier, 2 + (nx - 1) + (n_col - 1))

    forward(k)
    cross(0)
    bias[...] = jnp.zeros_like(bias)
    for s in range(n_col):
        if s % 2:

            @pl.when(s <= 2 * low)
            def _():
                arrive(s)
                if s + 1 < n_col:
                    arrive(s + 1)

        if s:
            pl.when(s > 2 * low)(functools.partial(arrive, s))
        project(s, 0)
        if s >= 1:
            finish(s - 1)
        project(s, 1)
        pair_sum(s)
        if s >= 2:
            back(s - 2)
        if s >= 1:
            relay(s - 1)
            cross(s)
        if s >= 2:
            relay_last(s - 2)
    for arr in (0, 1):
        keep(ins[arr].at[pl.ds(0, n_col)], ins_out[arr].at[pl.ds(0, n_col)], o_in.at[arr, n_col])
    finish(n_col - 1)
    if n_col >= 2:
        back(n_col - 2)
        relay_last(n_col - 2)
    relay(n_col - 1)
    back(n_col - 1)
    relay_last(n_col - 1)

    for s in range(n_col):
        b = which(s)
        for arr in (1, 0):
            for i in range(nx):
                at = 2 * origin(i) + (1 - core)
                if arr == 0:
                    got(outs[arr].at[b, at], r_sib.at[s, arr, i])
                got(outs[arr].at[n_col + b, at], r_sib.at[s, arr, nx + i])
            keep(outs[arr].at[b], outs_out[arr].at[b], o_mid.at[s, arr, 0])
            keep(outs[arr].at[n_col + b], outs_out[arr].at[n_col + b], o_mid.at[s, arr, 1])
        add_bias(n_col + b)

    total = share[0].astype(jnp.float32)
    for s in range(1, n_col):
        b = which(s)
        remote(share.at[s], shares.at[b], s_share.at[s], r_share.at[b], col=b).wait_recv()
        total = total + shares[b].astype(jnp.float32)
    d_out[...] = total.astype(jnp.bfloat16)

    for b in range(n_col):
        for arr in (0, 1):
            deep(arr, b).wait()
            keep(ins[arr].at[n_col + b], ins_out[arr].at[n_col + b], o_in.at[arr, b])

            @pl.when(jnp.logical_and(b <= k, k < n_col - 1))
            def _():
                line(arr, b, True).wait_send()

            @pl.when(jnp.logical_and(b >= k, k > 0))
            def _():
                line(arr, b, False).wait_send()

    for copy in sent:
        copy.wait_send()
    for copy in kept:
        copy.wait()


def exchange(n_row, n_col, inputs, cotangent, w_in, w_out, b_in):
    block, width = inputs.shape
    hidden = w_in.shape[1]
    nx, sub = n_row // 2, block // n_row
    kind = jnp.bfloat16
    wide = jax.ShapeDtypeStruct((2 * n_col, block, width), kind)
    deep = jax.ShapeDtypeStruct((2 * n_col, n_row, sub, hidden), kind)
    vmem, hbm = pl.BlockSpec(memory_space=pltpu.VMEM), pl.BlockSpec(memory_space=pl.ANY)
    sem = lambda *shape: pltpu.SemaphoreType.DMA(shape)
    flops = 6 * n_col * block * width * hidden
    return pl.pallas_call(
        functools.partial(kernel, n_row, n_col),
        out_shape=(wide, wide, deep, deep, jax.ShapeDtypeStruct((block, width), kind), jax.ShapeDtypeStruct((1, hidden), jnp.float32)),
        in_specs=[vmem, vmem, hbm, hbm, vmem],
        out_specs=(hbm,) * 4 + (vmem, vmem),
        scratch_shapes=[pltpu.VMEM(a.shape, kind) for a in (wide, wide, deep, deep, w_in, w_out)]
        + [
            pltpu.VMEM((n_col, 2, 2, nx, sub, hidden), kind),
            pltpu.VMEM((n_col, 2, nx, sub, hidden), kind),
            pltpu.VMEM((n_col, 2, nx - 1, sub, hidden), kind),
            pltpu.VMEM((n_col, block, width), kind),
            pltpu.VMEM((n_col, block, width), kind),
        ]
        + [sem(2, n_col)] * 5
        + [sem(n_col, 2)] * 2
        + [sem(n_col, 2, nx - 1)] * 2
        + [sem(n_col, 2, nx - 1)] * 2
        + [sem(n_col, 2)] * 2
        + [sem(n_col, 2, nx - 1)] * 2
        + [sem(n_col, 2, 2 * nx)] * 2
        + [sem(n_col)] * 2
        + [sem(2), sem(2, n_col + 1), sem(n_col, 2, 2)],
        compiler_params=pltpu.CompilerParams(
            collective_id=0, has_side_effects=True, vmem_limit_bytes=60 * 2**20
        ),
        cost_estimate=pl.CostEstimate(
            flops=flops, bytes_accessed=4 * width * hidden, transcendentals=block * hidden
        ),
    )(inputs, cotangent, w_in, w_out, b_in)


def on_device(n_row, n_col, normed, positions, cotangent, w_in, b_in, w_out):
    width, hidden = w_in.shape
    first = lax.axis_index("row") * width
    inputs = (normed.astype(jnp.float32) + sincos(positions, first, width)).astype(jnp.bfloat16)
    x_all, c_all, a_all, g_all, d_normed, d_b_in = exchange(
        n_row, n_col, inputs, cotangent, w_in, w_out, b_in.reshape(1, hidden)
    )
    rows = x_all.shape[0] * x_all.shape[1]
    grads = g_all.reshape(rows, hidden)
    contract = (((0,), (0,)), ((), ()))
    d_w_out = lax.dot_general(
        a_all.reshape(rows, hidden), c_all.reshape(rows, width), contract,
        preferred_element_type=jnp.float32,
    )
    d_w_in = lax.dot_general(
        x_all.reshape(rows, width), grads, contract, preferred_element_type=jnp.float32
    )
    return (d_normed, d_w_in, d_b_in.reshape(hidden), d_w_out)


def solution(mesh):
    placed = (
        P(("depth", "col"), "row"),
        P(("depth", "col")),
        P(("depth", "col"), "row"),
        P("row", "col"),
        P("col"),
        P("col", "row"),
    )
    return jax.shard_map(
        functools.partial(on_device, mesh.shape["row"], mesh.shape["col"]),
        mesh=mesh,
        in_specs=placed,
        out_specs=(P(("depth", "col"), "row"), P("row", "col"), P("col"), P("col", "row")),
        check_vma=False,
    )
```

```python
import functools
import math

import jax
import jax.numpy as jnp
from jax import lax
from jax.experimental import pallas as pl
from jax.experimental.pallas import tpu as pltpu
from jax.sharding import PartitionSpec as P

D = 6144
MESH = pl.DeviceIdType.MESH


coeff = 0.7978845608028654


def sincos(positions, first, width):
    places = positions.astype(jnp.float32)[:, None]
    column = first + jnp.arange(width, dtype=jnp.int32)
    expo = (2 * (column // 2)).astype(jnp.float32) / jnp.float32(D)
    freq = jnp.power(jnp.float32(10000.0), -expo)
    angle = places * freq[None, :]
    return jnp.where((column % 2 == 0)[None, :], jnp.sin(angle), jnp.cos(angle))


def gelu_pair(value):
    inner = coeff * (value + 0.044715 * value * value * value)
    slope = jnp.tanh(inner)
    out = 0.5 * value * (1.0 + slope)
    grad = 0.5 * (1.0 + slope) + 0.5 * value * (1.0 - slope * slope) * coeff * (
        1.0 + 3.0 * 0.044715 * value * value
    )
    return (out, grad)


def kernel(
    n_row, n_col,
    x_ref, c_ref, win_hbm, wout_hbm, b_ref,
    x_out, c_out, a_out, g_out, d_out, bias,
    x_all, c_all, a_all, g_all, win_ref, wout_ref,
    part, half, far, share, shares,
    s_right, s_left, r_line, s_deep, r_deep,
    s_pair, r_pair, s_far, r_far,
    s_gx, r_gx, s_gy, r_gy, s_gyx, r_gyx, s_sib, r_sib,
    s_share, r_share, w_sem, o_in, o_mid,
):
    d, r, k = lax.axis_index("depth"), lax.axis_index("row"), lax.axis_index("col")
    nx = n_row // 2
    px, core = lax.div(r, 2), lax.rem(r, 2)
    sib = 2 * px + (1 - core)
    other = 1 - d
    block, width = x_ref.shape
    hidden = win_ref.shape[1]
    sub = block // n_row
    tile = math.gcd(hidden, 768)
    tiles = hidden // tile
    low = jnp.minimum(k, n_col - 1 - k)
    ins, outs = (x_all, c_all), (a_all, g_all)
    ins_out, outs_out = (x_out, c_out), (a_out, g_out)
    sent, kept = [], []
    weights = [
        pltpu.make_async_copy(win_hbm, win_ref, w_sem.at[0]),
        pltpu.make_async_copy(wout_hbm, wout_ref, w_sem.at[1]),
    ]
    for copy in weights:
        copy.start()

    def keep(src, dst, sem):
        copy = pltpu.make_async_copy(src, dst, sem)
        copy.start()
        kept.append(copy)

    def peer(i):
        return lax.rem(px + i, nx)

    def origin(i):
        return lax.rem(px + nx - i, nx)

    def remote(src, dst, send, recv, **where):
        return pltpu.make_async_remote_copy(
            src_ref=src, dst_ref=dst, send_sem=send, recv_sem=recv,
            device_id=where, device_id_type=MESH,
        )

    def go(*args, **where):
        copy = remote(*args, **where)
        copy.start()
        sent.append(copy)

    def which(s):
        if s == 0:
            return k
        near = k - (s + 1) // 2 if s % 2 else k + s // 2
        rest = jnp.where(2 * k < n_col - 1, k + (s - low), k - (s - low))
        return jnp.where(s <= 2 * low, near, rest)

    def line(arr, b, right):
        ref = ins[arr].at[b]
        if right:
            return remote(ref, ref, s_right.at[arr, b], r_line.at[arr, b], col=jnp.minimum(k + 1, n_col - 1))
        return remote(ref, ref, s_left.at[arr, b], r_line.at[arr, b], col=jnp.maximum(k - 1, 0))

    def deep(arr, b):
        return remote(ins[arr].at[b], ins[arr].at[n_col + b], s_deep.at[arr, b], r_deep.at[arr, b], depth=other)

    def forward(b):
        @pl.when(jnp.logical_and(b <= k, k < n_col - 1))
        def _():
            for arr in (0, 1):
                line(arr, b, True).start()

        @pl.when(jnp.logical_and(b >= k, k > 0))
        def _():
            for arr in (0, 1):
                line(arr, b, False).start()

    def cross(s):
        for arr in (0, 1):
            deep(arr, which(s)).start()

    def arrive(s):
        b = which(s)
        for arr in (0, 1):
            line(arr, b, True).wait_recv()
        forward(b)

    def project(s, *arrs):
        b = which(s)
        for arr in arrs:
            if s == 0:
                weights[arr].wait()

            def body(i, carry):
                cols = pl.ds(pl.multiple_of(i * tile, tile), tile)
                if arr == 0:
                    acc = jnp.dot(x_all[b], win_ref[:, cols], preferred_element_type=jnp.float32)
                else:
                    acc = lax.dot_general(
                        c_all[b], wout_ref[cols, :], (((1,), (1,)), ((), ())),
                        preferred_element_type=jnp.float32,
                    )
                acc = acc.astype(jnp.bfloat16)
                for p in range(nx):
                    for q in (0, 1):
                        at = (2 * p + q) * sub
                        part[s, arr, q, p, :, cols] = acc[at : at + sub]
                return carry

            lax.fori_loop(0, tiles, body, 0)
            go(part.at[s, arr, 1 - core], half.at[s, arr], s_pair.at[s, arr], r_pair.at[s, arr], row=sib)

    def pair_sum(s, *arrs):
        for arr in arrs:
            remote(
                part.at[s, arr, 1 - core], half.at[s, arr], s_pair.at[s, arr], r_pair.at[s, arr], row=sib
            ).wait_recv()

            def body(i, carry):
                cols = pl.ds(pl.multiple_of(i * tile, tile), tile)
                for p in range(nx):
                    mine = part[s, arr, core, p, :, cols].astype(jnp.float32)
                    theirs = half[s, arr, p, :, cols].astype(jnp.float32)
                    half[s, arr, p, :, cols] = (mine + theirs).astype(jnp.bfloat16)
                return carry

            lax.fori_loop(0, tiles, body, 0)
            for i in range(1, nx):
                go(
                    half.at[s, arr, peer(i)], far.at[s, arr, i - 1],
                    s_far.at[s, arr, i - 1], r_far.at[s, arr, i - 1], row=2 * peer(i) + core,
                )

    def finish(s):
        b = which(s)
        for arr in (0, 1):
            for i in range(1, nx):
                remote(
                    half.at[s, arr, peer(i)], far.at[s, arr, i - 1],
                    s_far.at[s, arr, i - 1], r_far.at[s, arr, i - 1], row=2 * peer(i) + core,
                ).wait_recv()

        def body(i, carry):
            cols = pl.ds(pl.multiple_of(i * tile, tile), tile)
            total = []
            for arr in (0, 1):
                value = half[s, arr, px, :, cols].astype(jnp.float32)
                for j in range(1, nx):
                    value = value + far[s, arr, j - 1, :, cols].astype(jnp.float32)
                total.append(value)
            act, slope = gelu_pair(total[0] + b_ref[:, cols])
            a_all[b, r, :, cols] = act.astype(jnp.bfloat16)
            g_all[b, r, :, cols] = (total[1] * slope).astype(jnp.bfloat16)
            return carry

        lax.fori_loop(0, tiles, body, 0)
        for arr in (1, 0):
            own = outs[arr].at[b, r]
            go(own, outs[arr].at[n_col + b, r], s_gy.at[s, arr], r_gy.at[s, arr], depth=other)
        for arr in (1, 0):
            own = outs[arr].at[b, r]
            for i in range(1, nx):
                go(own, own, s_gx.at[s, arr, i - 1], r_gx.at[s, arr, i - 1], row=2 * peer(i) + core)
            go(own, own, s_sib.at[s, arr, 0], r_sib.at[s, arr, 0], row=sib)

    def got(ref, recv):
        remote(ref, ref, s_sib.at[0, 0, 0], recv, row=sib).wait_recv()

    def relay(s):
        b = which(s)
        for arr in (1, 0):
            far_own = outs[arr].at[n_col + b, r]
            got(far_own, r_gy.at[s, arr])
            for i in range(1, nx):
                go(far_own, far_own, s_gyx.at[s, arr, i - 1], r_gyx.at[s, arr, i - 1], row=2 * peer(i) + core)
            go(far_own, far_own, s_sib.at[s, arr, nx], r_sib.at[s, arr, nx], row=sib)
        for arr in (1, 0):
            for i in range(1, nx):
                piece = outs[arr].at[b, 2 * origin(i) + core]
                got(piece, r_gx.at[s, arr, i - 1])
                go(piece, piece, s_sib.at[s, arr, i], r_sib.at[s, arr, i], row=sib)

    def relay_last(s):
        b = which(s)
        for arr in (1, 0):
            for i in range(1, nx):
                piece = outs[arr].at[n_col + b, 2 * origin(i) + core]
                got(piece, r_gyx.at[s, arr, i - 1])
                go(piece, piece, s_sib.at[s, arr, nx + i], r_sib.at[s, arr, nx + i], row=sib)

    def add_bias(b):
        def body(i, carry):
            cols = pl.ds(pl.multiple_of(i * tile, tile), tile)
            rows = g_all[b, :, :, cols].astype(jnp.float32).reshape(block, tile)
            bias[:, cols] += jnp.sum(rows, axis=0, keepdims=True)
            return carry

        lax.fori_loop(0, tiles, body, 0)

    def back(s):
        b = which(s)
        for i in range(nx):
            got(g_all.at[b, 2 * origin(i) + (1 - core)], r_sib.at[s, 1, i])
        step = math.gcd(width, 768)

        def body(i, carry):
            cols = pl.ds(pl.multiple_of(i * step, step), step)
            acc = lax.dot_general(
                g_all[b].reshape(block, hidden), win_ref[cols, :], (((1,), (1,)), ((), ())),
                preferred_element_type=jnp.float32,
            )
            share[s, :, cols] = acc.astype(jnp.bfloat16)
            return carry

        lax.fori_loop(0, width // step, body, 0)
        add_bias(b)
        if s:
            go(share.at[s], shares.at[k], s_share.at[s], r_share.at[k], col=b)

    barrier = pltpu.get_barrier_semaphore()
    pl.semaphore_signal(barrier, inc=1, device_id={"row": sib}, device_id_type=MESH)
    pl.semaphore_signal(barrier, inc=1, device_id={"depth": other}, device_id_type=MESH)
    for i in range(1, nx):
        pl.semaphore_signal(barrier, inc=1, device_id={"row": 2 * peer(i) + core}, device_id_type=MESH)

    for i in range(1, n_col):
        pl.semaphore_signal(barrier, inc=1, device_id={"col": lax.rem(k + i, n_col)}, device_id_type=MESH)

    x_all[k] = x_ref[...]
    c_all[k] = c_ref[...]
    pl.semaphore_wait(barrier, 2 + (nx - 1) + (n_col - 1))

    forward(k)
    cross(0)
    bias[...] = jnp.zeros_like(bias)
    for s in range(n_col):
        if s % 2:

            @pl.when(s <= 2 * low)
            def _():
                arrive(s)
                if s + 1 < n_col:
                    arrive(s + 1)

        if s:
            pl.when(s > 2 * low)(functools.partial(arrive, s))
        project(s, 0)
        if s >= 1:
            finish(s - 1)
            pair_sum(s, 0)
        project(s, 1)
        if s == 0:
            pair_sum(s, 0)
        pair_sum(s, 1)
        if s >= 2:
            back(s - 2)
        if s >= 1:
            relay(s - 1)
            cross(s)
        if s >= 2:
            relay_last(s - 2)
    for arr in (0, 1):
        keep(ins[arr].at[pl.ds(0, n_col)], ins_out[arr].at[pl.ds(0, n_col)], o_in.at[arr, n_col])
    finish(n_col - 1)
    if n_col >= 2:
        back(n_col - 2)
        relay_last(n_col - 2)
    relay(n_col - 1)
    back(n_col - 1)
    relay_last(n_col - 1)

    for s in range(n_col):
        b = which(s)
        for arr in (1, 0):
            for i in range(nx):
                at = 2 * origin(i) + (1 - core)
                if arr == 0:
                    got(outs[arr].at[b, at], r_sib.at[s, arr, i])
                got(outs[arr].at[n_col + b, at], r_sib.at[s, arr, nx + i])
            keep(outs[arr].at[b], outs_out[arr].at[b], o_mid.at[s, arr, 0])
            keep(outs[arr].at[n_col + b], outs_out[arr].at[n_col + b], o_mid.at[s, arr, 1])
        add_bias(n_col + b)

    total = share[0].astype(jnp.float32)
    for s in range(1, n_col):
        b = which(s)
        remote(share.at[s], shares.at[b], s_share.at[s], r_share.at[b], col=b).wait_recv()
        total = total + shares[b].astype(jnp.float32)
    d_out[...] = total.astype(jnp.bfloat16)

    for b in range(n_col):
        for arr in (0, 1):
            deep(arr, b).wait()
            keep(ins[arr].at[n_col + b], ins_out[arr].at[n_col + b], o_in.at[arr, b])

            @pl.when(jnp.logical_and(b <= k, k < n_col - 1))
            def _():
                line(arr, b, True).wait_send()

            @pl.when(jnp.logical_and(b >= k, k > 0))
            def _():
                line(arr, b, False).wait_send()

    for copy in sent:
        copy.wait_send()
    for copy in kept:
        copy.wait()


def exchange(n_row, n_col, inputs, cotangent, w_in, w_out, b_in):
    block, width = inputs.shape
    hidden = w_in.shape[1]
    nx, sub = n_row // 2, block // n_row
    kind = jnp.bfloat16
    wide = jax.ShapeDtypeStruct((2 * n_col, block, width), kind)
    deep = jax.ShapeDtypeStruct((2 * n_col, n_row, sub, hidden), kind)
    vmem, hbm = pl.BlockSpec(memory_space=pltpu.VMEM), pl.BlockSpec(memory_space=pl.ANY)
    sem = lambda *shape: pltpu.SemaphoreType.DMA(shape)
    flops = 6 * n_col * block * width * hidden
    return pl.pallas_call(
        functools.partial(kernel, n_row, n_col),
        out_shape=(wide, wide, deep, deep, jax.ShapeDtypeStruct((block, width), kind), jax.ShapeDtypeStruct((1, hidden), jnp.float32)),
        in_specs=[vmem, vmem, hbm, hbm, vmem],
        out_specs=(hbm,) * 4 + (vmem, vmem),
        scratch_shapes=[pltpu.VMEM(a.shape, kind) for a in (wide, wide, deep, deep, w_in, w_out)]
        + [
            pltpu.VMEM((n_col, 2, 2, nx, sub, hidden), kind),
            pltpu.VMEM((n_col, 2, nx, sub, hidden), kind),
            pltpu.VMEM((n_col, 2, nx - 1, sub, hidden), kind),
            pltpu.VMEM((n_col, block, width), kind),
            pltpu.VMEM((n_col, block, width), kind),
        ]
        + [sem(2, n_col)] * 5
        + [sem(n_col, 2)] * 2
        + [sem(n_col, 2, nx - 1)] * 2
        + [sem(n_col, 2, nx - 1)] * 2
        + [sem(n_col, 2)] * 2
        + [sem(n_col, 2, nx - 1)] * 2
        + [sem(n_col, 2, 2 * nx)] * 2
        + [sem(n_col)] * 2
        + [sem(2), sem(2, n_col + 1), sem(n_col, 2, 2)],
        compiler_params=pltpu.CompilerParams(
            collective_id=0, has_side_effects=True, vmem_limit_bytes=60 * 2**20
        ),
        cost_estimate=pl.CostEstimate(
            flops=flops, bytes_accessed=4 * width * hidden, transcendentals=block * hidden
        ),
    )(inputs, cotangent, w_in, w_out, b_in)


def on_device(n_row, n_col, normed, positions, cotangent, w_in, b_in, w_out):
    width, hidden = w_in.shape
    first = lax.axis_index("row") * width
    inputs = (normed.astype(jnp.float32) + sincos(positions, first, width)).astype(jnp.bfloat16)
    x_all, c_all, a_all, g_all, d_normed, d_b_in = exchange(
        n_row, n_col, inputs, cotangent, w_in, w_out, b_in.reshape(1, hidden)
    )
    rows = x_all.shape[0] * x_all.shape[1]
    grads = g_all.reshape(rows, hidden)
    contract = (((0,), (0,)), ((), ()))
    d_w_out = lax.dot_general(
        a_all.reshape(rows, hidden), c_all.reshape(rows, width), contract,
        preferred_element_type=jnp.float32,
    )
    d_w_in = lax.dot_general(
        x_all.reshape(rows, width), grads, contract, preferred_element_type=jnp.float32
    )
    return (d_normed, d_w_in, d_b_in.reshape(hidden), d_w_out)


def solution(mesh):
    placed = (
        P(("depth", "col"), "row"),
        P(("depth", "col")),
        P(("depth", "col"), "row"),
        P("row", "col"),
        P("col"),
        P("col", "row"),
    )
    return jax.shard_map(
        functools.partial(on_device, mesh.shape["row"], mesh.shape["col"]),
        mesh=mesh,
        in_specs=placed,
        out_specs=(P(("depth", "col"), "row"), P("row", "col"), P("col"), P("col", "row")),
        check_vma=False,
    )
```
